32 devices in a mesh: groups: 2 (over x), seq: 16 (over z, y, core).
Axes of the slice: x: 2, y: 2, z: 4, core: 2. Of those that a mesh axis runs over, the one named last changes fastest.
Arguments:
- q_tokens: bfloat16 [4096, 2048], P(('groups', 'seq')), parts along dimension 0, may hold values from -44 to 44
- k_tokens: bfloat16 [4096, 2048], P(('groups', 'seq')), parts along dimension 0, may hold values from -4 to 4
- v_tokens: bfloat16 [4096, 2048], P(('groups', 'seq')), parts along dimension 0, may hold values from -6 to 6
- dout_tokens: bfloat16 [4096, 2048], P(('groups', 'seq')), parts along dimension 0, may hold values from -6 to 6
- q_beacons: bfloat16 [128, 2048], P(('groups', 'seq')), parts along dimension 0, may hold values from -44 to 44
- k_beacons: bfloat16 [128, 2048], P(('groups', 'seq')), parts along dimension 0, may hold values from -4 to 4
- v_beacons: bfloat16 [128, 2048], P(('groups', 'seq')), parts along dimension 0, may hold values from -6 to 6
- dout_beacons: bfloat16 [128, 2048], P(('groups', 'seq')), parts along dimension 0, may hold values from -6 to 6
- block_mask: int32 [32, 16], P(('groups', 'seq')), parts along dimension 0, may hold values 0 or 1
- beacon_offsets: int32 [128], P(('groups', 'seq')), parts along dimension 0, may hold values from 0 to 31
Outputs:
- out_tokens: bfloat16 [4096, 2048], P(('groups', 'seq')), parts along dimension 0
- out_beacons: bfloat16 [128, 2048], P(('groups', 'seq')), parts along dimension 0
- grad_q_tokens: bfloat16 [4096, 2048], P(('groups', 'seq')), parts along dimension 0
- grad_k_tokens: bfloat16 [4096, 2048], P(('groups', 'seq')), parts along dimension 0
- grad_v_tokens: bfloat16 [4096, 2048], P(('groups', 'seq')), parts along dimension 0
- grad_q_beacons: bfloat16 [128, 2048], P(('groups', 'seq')), parts along dimension 0
- grad_k_beacons: bfloat16 [128, 2048], P(('groups', 'seq')), parts along dimension 0
- grad_v_beacons: bfloat16 [128, 2048], P(('groups', 'seq')), parts along dimension 0
The draws below stay inside these ranges and needn't reach their ends.
There are 2 independent parts, one for each index of `groups`. The reference program is written for one: setup_inputs(seed, part) draws one part's arguments, and reference() takes and returns one part's arrays. A program takes and returns all parts, laid end to end along the dimension named above; each array names one. Nothing has to cross between parts.
All inputs are finite; a program needn't handle non-finite values. No bound on the sum of `block_mask` on one device may be relied on, other than what follows from the above.
Results may differ from the reference program's by a relative error of at most 0.015.
The reference program's roundings to bfloat16 on the way (of `weights` and `dscores`) count: a program that leaves them out, or rounds other values in their place, can miss the bound.
Values may be sent and summed in bfloat16 or wider, within the bound.
A program may use at most 128 MiB of HBM per device.

```python
import jax
import jax.numpy as jnp
from jax import lax

SEG = 128
HEADS = 16
HEAD_DIM = 128
RATIO = 32
NB = 4
NSEG = 16
TOKENS = 2048
BEACONS = 64
N_SEQ = 16


def fresh_values(key, rows_total, cols_total):
    return jnp.clip(jax.random.normal(key, (rows_total, cols_total), jnp.float32), -4.0, 4.0)


def token_keys(key):
    base_rows = fresh_values(jax.random.fold_in(key, 101), TOKENS, HEADS * HEAD_DIM)
    return base_rows


def beacon_keys(key):
    base_rows = fresh_values(jax.random.fold_in(key, 303), BEACONS, HEADS * HEAD_DIM)
    return base_rows


def draw_k_tokens(key, part):
    return token_keys(key).astype(jnp.bfloat16)


def draw_q_tokens(key, part):
    queries = fresh_values(jax.random.fold_in(key, 202), TOKENS, HEADS * HEAD_DIM)
    return queries.astype(jnp.bfloat16)


def draw_k_beacons(key, part):
    return beacon_keys(key).astype(jnp.bfloat16)


def draw_q_beacons(key, part):
    queries = fresh_values(jax.random.fold_in(key, 404), BEACONS, HEADS * HEAD_DIM)
    return queries.astype(jnp.bfloat16)


def plant(result, own_key, smallest, top_value):
    longest = result.shape.index(max(result.shape))
    spots = []
    for shift in (0, 1):
        where = [jax.random.randint(jax.random.fold_in(own_key, axis), (), 0, length) for axis, length in enumerate(result.shape)]
        where[longest] = (where[longest] + shift) % result.shape[longest]
        spots.append(tuple(where))
    return result.at[spots[0]].set(smallest).at[spots[1]].set(top_value)


def shard_levels(key, shape, split, smallest, largest):
    level = 1.0
    for axis_at, shards_of in split:
        heights = jax.random.uniform(jax.random.fold_in(jax.random.fold_in(key, 6), axis_at), (shards_of,), jnp.float32, smallest / len(split), largest / len(split))
        level = level * jnp.repeat(jnp.exp(heights), shape[axis_at] // shards_of).reshape((-1,) + (1,) * (len(shape) - 1 - axis_at))
    return level


def noise(rng, extent, deviation, most, pieces=(), kind=jnp.bfloat16):
    factor_of = shard_levels(rng, extent, pieces, -0.22, 0.18) if pieces else 1.0
    values = jax.random.normal(rng, extent, jnp.float32) * deviation * factor_of
    return jnp.minimum(jnp.maximum(values, -most), most).astype(kind)


def setup_inputs(seed: int = 0, part: int = 0) -> dict:
    key_of = jax.random.split(jax.random.key(seed), 11)
    part_splits = jax.random.split(jax.random.fold_in(key_of[10], part), 11)
    q_tokens = draw_q_tokens(jax.random.fold_in(jax.random.fold_in(key_of[10], part), 71), part)
    k_tokens = draw_k_tokens(jax.random.fold_in(jax.random.fold_in(key_of[10], part), 71), part)
    v_tokens = noise(part_splits[2], (TOKENS, HEADS * HEAD_DIM), 1.0, 6.0, ((0, 16),))
    dout_tokens = noise(part_splits[3], (TOKENS, HEADS * HEAD_DIM), 1.0, 6.0, ((0, 16),))
    q_beacons = draw_q_beacons(jax.random.fold_in(jax.random.fold_in(key_of[10], part), 71), part)
    k_beacons = draw_k_beacons(jax.random.fold_in(jax.random.fold_in(key_of[10], part), 71), part)
    v_beacons = noise(part_splits[6], (BEACONS, HEADS * HEAD_DIM), 1.0, 6.0, ((0, 16),))
    dout_beacons = noise(part_splits[7], (BEACONS, HEADS * HEAD_DIM), 1.0, 6.0, ((0, 16),))
    block_mask = plant((jax.random.randint(part_splits[8], (NSEG, NSEG), 0, 2) < 1).astype(jnp.int32), jax.random.fold_in(part_splits[8], 1), 0, 1)
    beacon_offsets = plant(jax.random.randint(part_splits[9], (BEACONS,), 0, RATIO), jax.random.fold_in(part_splits[9], 1), 0, RATIO - 1).astype(jnp.int32)
    return {"q_tokens": q_tokens, "k_tokens": k_tokens, "v_tokens": v_tokens, "dout_tokens": dout_tokens, "q_beacons": q_beacons, "k_beacons": k_beacons, "v_beacons": v_beacons, "dout_beacons": dout_beacons, "block_mask": block_mask, "beacon_offsets": beacon_offsets}


def visible(seg_index, mask_row, offsets, seg_len, beacon_count, window, segments):
    ratio = seg_len // beacon_count
    rows_total = seg_len + beacon_count
    query_ids = jnp.arange(rows_total, dtype=jnp.int32)[:, None]
    is_raw = query_ids < seg_len
    beacon_id = query_ids - seg_len
    limit = jnp.concatenate([jnp.zeros((seg_len,), jnp.int32), jnp.arange(beacon_count, dtype=jnp.int32) * ratio + offsets.astype(jnp.int32)])[:, None]
    key_ids = jnp.arange(window + seg_len + segments * beacon_count, dtype=jnp.int32)[None, :]
    in_window = key_ids < window
    in_own = (key_ids >= window) & (key_ids < window + seg_len)
    lag_own = query_ids - (key_ids - window)
    flat_id = key_ids - window - seg_len
    owner = flat_id // beacon_count
    slot_id = flat_id % beacon_count
    opened = jnp.concatenate([jnp.zeros((window + seg_len,), jnp.int32), jnp.repeat(mask_row.astype(jnp.int32), beacon_count)])[None, :] == 1
    earlier = (flat_id >= 0) & (owner < seg_index) & opened
    raw_ok = (in_window & (key_ids > query_ids) & (seg_index >= 1)) | (in_own & (lag_own >= 0) & (lag_own < window)) | earlier
    beacon_ok = (in_own & (key_ids - window <= limit)) | earlier | ((flat_id >= 0) & (owner == seg_index) & (slot_id <= beacon_id))
    return jnp.where(is_raw, raw_ok, beacon_ok)


def attend(queries, key_rows, values, grads_out, allowed, score_scale):
    q32 = queries.astype(jnp.float32)
    k32 = key_rows.astype(jnp.float32)
    v32 = values.astype(jnp.float32)
    g32 = grads_out.astype(jnp.float32)
    scores = jnp.einsum("qhd,khd->hqk", q32, k32) * score_scale
    scores = jnp.where(allowed[None], scores, -jnp.inf)
    row_max = jnp.max(scores, axis=2, keepdims=True)
    exp_scores = jnp.exp(scores - row_max)
    prob_rows = exp_scores / jnp.sum(exp_scores, axis=2, keepdims=True)
    weights = lax.optimization_barrier(prob_rows.astype(jnp.bfloat16))
    output = jnp.einsum("hqk,khd->qhd", weights.astype(jnp.float32), v32).astype(jnp.bfloat16)
    out_kept = lax.optimization_barrier(output)
    row_delta = jnp.sum(g32 * out_kept.astype(jnp.float32), axis=2)
    grad_prob = jnp.einsum("qhd,khd->hqk", g32, v32)
    dscores = lax.optimization_barrier((prob_rows * (grad_prob - row_delta.T[:, :, None])).astype(jnp.bfloat16))
    ds32 = dscores.astype(jnp.float32)
    grad_q = (jnp.einsum("hqk,khd->qhd", ds32, k32) * score_scale).astype(jnp.bfloat16)
    grad_k = jnp.einsum("hqk,qhd->khd", ds32, q32) * score_scale
    grad_v = jnp.einsum("hqk,qhd->khd", weights.astype(jnp.float32), g32)
    return output, grad_q, grad_k, grad_v


def reference(q_tokens, k_tokens, v_tokens, dout_tokens, q_beacons, k_beacons, v_beacons, dout_beacons, block_mask, beacon_offsets):
    feat_width = HEADS * HEAD_DIM
    window = SEG // 2
    score_scale = 1.0 / (HEAD_DIM ** 0.5)
    rows_total = SEG + NB

    def per_segment(matrix):
        return matrix.reshape(N_SEQ, SEG, feat_width)

    q_seg = per_segment(q_tokens)
    k_seg = per_segment(k_tokens)
    v_seg = per_segment(v_tokens)
    d_seg = per_segment(dout_tokens)
    tail_k = jnp.concatenate([jnp.zeros((1, window, feat_width), jnp.bfloat16), k_seg[:-1, SEG - window:]], axis=0)
    tail_v = jnp.concatenate([jnp.zeros((1, window, feat_width), jnp.bfloat16), v_seg[:-1, SEG - window:]], axis=0)
    bq_seg = q_beacons.reshape(N_SEQ, NB, feat_width)
    bd_seg = dout_beacons.reshape(N_SEQ, NB, feat_width)
    off_seg = beacon_offsets.reshape(N_SEQ, NB)
    seg_ids = jnp.arange(N_SEQ, dtype=jnp.int32)

    def segment_step(carry, inputs_now):
        seg_index, q_now, k_now, v_now, d_now, tk_now, tv_now, bq_now, bd_now, mask_now, off_now = inputs_now
        queries = jnp.concatenate([q_now, bq_now], axis=0)
        key_rows = jnp.concatenate([tk_now, k_now, k_beacons], axis=0)
        values = jnp.concatenate([tv_now, v_now, v_beacons], axis=0)
        grads_out = jnp.concatenate([d_now, bd_now], axis=0)
        allowed = visible(seg_index, mask_now, off_now, SEG, NB, window, N_SEQ)
        key_total = key_rows.shape[0]
        output, grad_q, grad_k, grad_v = attend(queries.reshape(rows_total, HEADS, HEAD_DIM), key_rows.reshape(key_total, HEADS, HEAD_DIM), values.reshape(key_total, HEADS, HEAD_DIM), grads_out.reshape(rows_total, HEADS, HEAD_DIM), allowed, score_scale)
        output = output.reshape(rows_total, feat_width)
        grad_q = grad_q.reshape(rows_total, feat_width)
        grad_k = grad_k.reshape(key_total, feat_width)
        grad_v = grad_v.reshape(key_total, feat_width)
        new_carry = (carry[0] + grad_k[window + SEG:], carry[1] + grad_v[window + SEG:])
        return new_carry, (output[:SEG], output[SEG:], grad_q[:SEG], grad_q[SEG:], grad_k[window:window + SEG], grad_v[window:window + SEG], grad_k[:window], grad_v[:window])

    zero_carry = (jnp.zeros((BEACONS, feat_width), jnp.float32), jnp.zeros((BEACONS, feat_width), jnp.float32))
    totals, outs_all = lax.scan(segment_step, zero_carry, (seg_ids, q_seg, k_seg, v_seg, d_seg, tail_k, tail_v, bq_seg, bd_seg, block_mask, off_seg))
    out_tok, out_bea, gq_tok, gq_bea, gk_own, gv_own, gk_win, gv_win = outs_all
    next_k = jnp.concatenate([gk_win[1:], jnp.zeros((1, window, feat_width), jnp.float32)], axis=0)
    next_v = jnp.concatenate([gv_win[1:], jnp.zeros((1, window, feat_width), jnp.float32)], axis=0)
    gk_tok = jnp.concatenate([gk_own[:, :SEG - window], gk_own[:, SEG - window:] + next_k], axis=1)
    gv_tok = jnp.concatenate([gv_own[:, :SEG - window], gv_own[:, SEG - window:] + next_v], axis=1)
    return (out_tok.reshape(TOKENS, feat_width), out_bea.reshape(BEACONS, feat_width), gq_tok.reshape(TOKENS, feat_width), gk_tok.reshape(TOKENS, feat_width).astype(jnp.bfloat16), gv_tok.reshape(TOKENS, feat_width).astype(jnp.bfloat16), gq_bea.reshape(BEACONS, feat_width), totals[0].astype(jnp.bfloat16), totals[1].astype(jnp.bfloat16))
```

```python
import functools
import math

import jax
import jax.numpy as jnp
from jax import lax
from jax.experimental import pallas as pl
from jax.experimental.pallas import tpu as pltpu
from jax.sharding import PartitionSpec as P

HEAD_DIM = 128
PAD = 16
MESH = pl.DeviceIdType.MESH
F32 = jnp.float32
BF16 = jnp.bfloat16


def dot(a, b, ca, cb):
    return lax.dot_general(a, b, (((ca,), (cb,)), ((), ())), preferred_element_type=F32)


def kernel(
    n, A, B, C, heads, seg, nb, win,
    q_ref, k_ref, v_ref, d_ref, qb_ref, kb_ref, vb_ref, db_ref, mask_ref, off_ref,
    o_t, o_b, gq_t, gk_t, gv_t, gq_b, gk_b, gv_b,
    G, KB, VB, TK, TV, SK, SV, RK, RV, WK, WV, QP, DP, bias,
    R, R1, S2, R2, X2, S3, R3,
    t_s, t_r, u_s, u_r, g1s, g1r, g2s, g2r, g3s, g3r, r1s, r1r, r2s, r2r, r3s, r3r,
):
    feat = heads * HEAD_DIM
    hc = heads // C
    hw = hc // 2
    w = hw * HEAD_DIM
    cw = hc * HEAD_DIM
    ratio = seg // nb
    rows = seg + PAD
    scale = 1.0 / HEAD_DIM**0.5
    me = lax.axis_index("seq")
    c0 = lax.rem(me, 2)
    b0 = lax.rem(me // 2, B)
    a0 = me // (2 * B)

    def at(a, b, c):
        return {"seq": (a * B + b) * 2 + c}

    def remote(src, dst, ss, rs, dev):
        return pltpu.make_async_remote_copy(
            src_ref=src, dst_ref=dst, send_sem=ss, recv_sem=rs, device_id=dev, device_id_type=MESH
        )

    zdev = [None] + [at(lax.rem(a0 + d, A), b0, c0) for d in range(1, A)]
    ydev = [None] + [at(a0, lax.rem(b0 + d, B), c0) for d in range(1, B)]
    cdev = at(a0, b0, 1 - c0)

    barrier = pltpu.get_barrier_semaphore()
    for dev in zdev[1:] + ydev[1:] + [cdev]:
        pl.semaphore_signal(barrier, inc=1, device_id=dev, device_id_type=MESH)

    @pl.when(me > 0)
    def _():
        pl.semaphore_signal(barrier, inc=1, device_id={"seq": me - 1}, device_id_type=MESH)

    @pl.when(me < n - 1)
    def _():
        pl.semaphore_signal(barrier, inc=1, device_id={"seq": me + 1}, device_id_type=MESH)

    for c in range(C):
        parts = []
        for half in range(2):
            cols = slice(c * cw + half * w, c * cw + (half + 1) * w)
            parts += [kb_ref[:, cols].astype(F32), vb_ref[:, cols].astype(F32)]
        G[c0, b0, a0, c] = jnp.concatenate(parts, axis=0).astype(BF16)

    pl.semaphore_wait(barrier, A + B + 1 - (me == 0).astype(jnp.int32) - (me == n - 1).astype(jnp.int32))

    for d in range(1, A):
        remote(G.at[c0, b0, a0], G.at[c0, b0, a0], g1s.at[d], g1r.at[d], zdev[d]).start()

    def tail(x, c):
        src, dst = ((k_ref, TK), (v_ref, TV))[x]
        cols = pl.ds(c * cw, cw)
        return remote(
            src.at[pl.ds(seg - win, win), cols], dst.at[:, cols], t_s.at[x, c], t_r.at[x, c], {"seq": lax.rem(me + 1, n)}
        )

    def back(x, c):
        src, dst = ((SK, RK), (SV, RV))[x]
        cols = pl.ds(c * cw, cw)
        return remote(
            src.at[:, cols], dst.at[:, cols], u_s.at[x, c], u_r.at[x, c], {"seq": lax.rem(me + n - 1, n)}
        )

    @pl.when(me < n - 1)
    def _():
        for c in range(C):
            tail(0, c).start()
            tail(1, c).start()

    @pl.when(me == 0)
    def _():
        TK[...] = jnp.zeros_like(TK)
        TV[...] = jnp.zeros_like(TV)

    @pl.when(me == n - 1)
    def _():
        RK[...] = jnp.zeros_like(RK)
        RV[...] = jnp.zeros_like(RV)

    zpad = jnp.zeros((PAD - nb, feat), F32)
    QP[...] = jnp.concatenate([qb_ref[...].astype(F32), zpad], axis=0).astype(BF16)
    DP[...] = jnp.concatenate([db_ref[...].astype(F32), zpad], axis=0).astype(BF16)

    NEG = -1e30

    def ids(width):
        return (
            lax.broadcasted_iota(jnp.int32, (rows, width), 0),
            lax.broadcasted_iota(jnp.int32, (rows, width), 1),
        )

    r, u = ids(win)
    ok = (r < seg) & (u > r) & (me >= 1)
    bias[:, :win] = jnp.where(ok, 0.0, NEG)
    r, u = ids(seg)
    limit = jnp.where(r < seg, r, -1)
    for b in range(nb):
        limit = jnp.where(r == seg + b, b * ratio + off_ref[b], limit)
    low = jnp.where(r < seg, r - win, -1)
    bias[:, win : win + seg] = jnp.where((u <= limit) & (u > low), 0.0, NEG)
    r, u = ids(n * nb)
    slot = u // nb
    half_n = n // 2
    owner = ((slot % A) * B + (slot % half_n) // A) * 2 + slot // half_n
    one = owner[:1]
    opened = jnp.zeros((1, n * nb), jnp.int32)
    for j in range(n):
        opened = jnp.where(one == j, mask_ref[0, j], opened)
    opened = jnp.where(one < me, opened, 0)
    earlier = jnp.broadcast_to(opened, (rows, n * nb)) == 1
    mine = (owner == me) & (r >= seg) & (u % nb <= r - seg)
    bias[:, win + seg :] = jnp.where((earlier | mine) & (r < seg + nb), 0.0, NEG)

    for d in range(1, A):
        remote(G.at[c0, b0, a0], G.at[c0, b0, lax.rem(a0 + A - d, A)], g1s.at[d], g1r.at[d], zdev[d]).wait_recv()
    for d in range(1, B):
        remote(G.at[c0, b0], G.at[c0, b0], g2s.at[d], g2r.at[d], ydev[d]).start()
    for d in range(1, B):
        remote(G.at[c0, b0], G.at[c0, lax.rem(b0 + B - d, B)], g2s.at[d], g2r.at[d], ydev[d]).wait_recv()
    remote(G.at[c0], G.at[c0], g3s.at[0], g3r.at[0], cdev).start()
    remote(G.at[c0], G.at[1 - c0], g3s.at[0], g3r.at[0], cdev).wait_recv()

    def assemble(m, carry):
        for c in range(C):
            for half in range(2):
                cols = slice(c * cw + half * w, c * cw + (half + 1) * w)
                got = []
                for i in range(PAD // nb):
                    s = m * (PAD // nb) + i
                    got.append(
                        G[s // half_n, (s % half_n) // A, s % A, c, half * 8 : half * 8 + 8, :].astype(F32)
                    )
                at_rows = pl.ds(pl.multiple_of(m * PAD, PAD), PAD)
                KB[at_rows, cols] = jnp.concatenate([x[:nb] for x in got], axis=0).astype(BF16)
                VB[at_rows, cols] = jnp.concatenate([x[nb:] for x in got], axis=0).astype(BF16)
        return carry

    lax.fori_loop(0, n * nb // PAD, assemble, 0)

    c_exp = scale * math.log2(math.e)

    def head(c, l):
        h = c * hc + l
        cols = pl.ds(pl.multiple_of(h * HEAD_DIM, HEAD_DIM), HEAD_DIM)
        q = jnp.concatenate([q_ref[:, cols], QP[:, cols]], axis=0)
        d = jnp.concatenate([d_ref[:, cols], DP[:, cols]], axis=0)
        kk = jnp.concatenate([TK[:, cols], k_ref[:, cols], KB[:, cols]], axis=0)
        vv = jnp.concatenate([TV[:, cols], v_ref[:, cols], VB[:, cols]], axis=0)
        s = dot(q, kk, 1, 1) + bias[...]
        gp = dot(d, vv, 1, 1)
        e = jnp.exp2((s - jnp.max(s, axis=1, keepdims=True)) * c_exp)
        p = e * (1.0 / jnp.sum(e, axis=1, keepdims=True))
        wt = p.astype(BF16)
        o = dot(wt, vv, 1, 0).astype(BF16)
        delta = jnp.sum(d.astype(F32) * o.astype(F32), axis=1, keepdims=True)
        ds = (p * (gp - delta)).astype(BF16)
        gq = (dot(ds, kk, 1, 0) * scale).astype(BF16)
        gv = dot(wt, d, 0, 0)
        gk = dot(ds, q, 0, 0) * scale
        o_t[:, cols] = o[:seg]
        o_b[:, cols] = o[seg : seg + nb]
        gq_t[:, cols] = gq[:seg]
        gq_b[:, cols] = gq[seg : seg + nb]
        mid = seg
        SK[:, cols] = gk[:win].astype(BF16)
        SV[:, cols] = gv[:win].astype(BF16)
        gk_t[: seg - win, cols] = gk[win:mid].astype(BF16)
        gv_t[: seg - win, cols] = gv[win:mid].astype(BF16)
        WK[:, cols] = gk[mid : win + seg]
        WV[:, cols] = gv[mid : win + seg]
        half = l // hw
        rcols = pl.ds(pl.multiple_of((l % hw) * HEAD_DIM, HEAD_DIM), HEAD_DIM)
        rrows = pl.ds(pl.multiple_of(half * 8, 8), 8)
        for sl in range(n):
            lo = win + seg + sl * nb
            both = jnp.concatenate([gk[lo : lo + nb], gv[lo : lo + nb]], axis=0)
            R[c, sl // half_n, (sl % half_n) // A, sl % A, rrows, rcols] = both

    def red1(c):
        return remote(R.at[c, 1 - c0], R1.at[c], r1s.at[c], r1r.at[c], cdev)

    def red2(c, d):
        return remote(S2.at[c, lax.rem(b0 + d, B)], R2.at[c, d], r2s.at[c, d], r2r.at[c, d], ydev[d])

    def red3(c, d):
        return remote(S3.at[c, lax.rem(a0 + d, A)], R3.at[c, d], r3s.at[c, d], r3r.at[c, d], zdev[d])

    def step1(c):
        red1(c).wait_recv()
        for b in range(B):
            tot = R1[c, b] + R[c, c0, b]
            R1[c, b] = tot
            S2[c, b] = tot.astype(BF16)
        for d in range(1, B):
            red2(c, d).start()

    def step2(c):
        tot = R1[c, b0]
        for d in range(1, B):
            red2(c, d).wait_recv()
            tot = tot + R2[c, d].astype(F32)
        X2[c] = tot
        S3[c] = tot.astype(BF16)
        for d in range(1, A):
            red3(c, d).start()

    def step3(c):
        tot = X2[c, a0]
        for d in range(1, A):
            red3(c, d).wait_recv()
            tot = tot + R3[c, d].astype(F32)
        for half in range(2):
            cols = slice(c * cw + half * w, c * cw + (half + 1) * w)
            gk_b[:, cols] = tot[half * 8 : half * 8 + nb].astype(BF16)
            gv_b[:, cols] = tot[half * 8 + nb : half * 8 + 8].astype(BF16)

    for c in range(C):

        @pl.when(me > 0)
        def _():
            tail(0, c).wait_recv()
            tail(1, c).wait_recv()

        def one_head(l, carry):
            head(c, l)
            return carry

        lax.fori_loop(0, hc, one_head, 0, unroll=UNROLL)

        red1(c).start()

        @pl.when(me > 0)
        def _():
            back(0, c).start()
            back(1, c).start()

        if c >= 1:
            step1(c - 1)
        if c >= 2:
            step2(c - 2)

    step1(C - 1)
    if C >= 2:
        step2(C - 2)
    step2(C - 1)

    for c in range(C):

        @pl.when(me < n - 1)
        def _():
            back(0, c).wait_recv()
            back(1, c).wait_recv()

        cols = slice(c * cw, (c + 1) * cw)
        gk_t[seg - win :, cols] = (WK[:, cols] + RK[:, cols].astype(F32)).astype(BF16)
        gv_t[seg - win :, cols] = (WV[:, cols] + RV[:, cols].astype(F32)).astype(BF16)

    for c in range(C):
        step3(c)

    for d in range(1, A):
        remote(G.at[c0, b0, a0], G.at[c0, b0, a0], g1s.at[d], g1r.at[d], zdev[d]).wait_send()
    for d in range(1, B):
        remote(G.at[c0, b0], G.at[c0, b0], g2s.at[d], g2r.at[d], ydev[d]).wait_send()
    remote(G.at[c0], G.at[c0], g3s.at[0], g3r.at[0], cdev).wait_send()
    for c in range(C):
        red1(c).wait_send()
        for d in range(1, B):
            red2(c, d).wait_send()
        for d in range(1, A):
            red3(c, d).wait_send()

        @pl.when(me < n - 1)
        def _():
            tail(0, c).wait_send()
            tail(1, c).wait_send()

        @pl.when(me > 0)
        def _():
            back(0, c).wait_send()
            back(1, c).wait_send()


UNROLL = 2


def per_device(n, q, k, v, dout, qb, kb, vb, db, mask, off):
    seg, feat = q.shape
    nb = qb.shape[0]
    win = seg // 2
    heads = feat // HEAD_DIM
    chips = n // 2
    B = 2 ** (int(math.log2(chips)) // 2)
    A = chips // B
    C = 4
    w = heads // C // 2 * HEAD_DIM
    keys = win + seg + n * nb
    vm = pltpu.VMEM
    dma = pltpu.SemaphoreType.DMA
    scratch = [
        vm((2, B, A, C, 16, w), BF16),
        vm((n * nb, feat), BF16),
        vm((n * nb, feat), BF16),
    ]
    scratch += [vm((win, feat), BF16)] * 6
    scratch += [vm((seg - win, feat), F32)] * 2
    scratch += [vm((PAD, feat), BF16)] * 2
    scratch += [vm((seg + PAD, keys), F32)]
    scratch += [
        vm((C, 2, B, A, 16, w), F32),
        vm((C, B, A, 16, w), F32),
        vm((C, B, A, 16, w), BF16),
        vm((C, B, A, 16, w), BF16),
        vm((C, A, 16, w), F32),
        vm((C, A, 16, w), BF16),
        vm((C, A, 16, w), BF16),
    ]
    scratch += [dma((2, C))] * 4 + [dma((A,))] * 2 + [dma((B,))] * 2 + [dma((1,))] * 2
    scratch += [dma((C,))] * 2 + [dma((C, B))] * 2 + [dma((C, A))] * 2
    big = jax.ShapeDtypeStruct((seg, feat), BF16)
    small = jax.ShapeDtypeStruct((nb, feat), BF16)
    vspec = pl.BlockSpec(memory_space=pltpu.VMEM)
    sspec = pl.BlockSpec(memory_space=pltpu.SMEM)
    macs = (seg + PAD) * keys * feat * 5
    return pl.pallas_call(
        functools.partial(kernel, n, A, B, C, heads, seg, nb, win),
        out_shape=(big, small, big, big, big, small, small, small),
        in_specs=[vspec] * 8 + [sspec] * 2,
        out_specs=(vspec,) * 8,
        scratch_shapes=scratch,
        cost_estimate=pl.CostEstimate(
            flops=2 * macs, bytes_accessed=8 * seg * feat * 2, transcendentals=(seg + PAD) * keys * heads
        ),
        compiler_params=pltpu.CompilerParams(
            collective_id=0, has_side_effects=True, vmem_limit_bytes=56 * 1024 * 1024
        ),
    )(q, k, v, dout, qb, kb, vb, db, mask, off)


def solution(mesh):
    rows = P(("groups", "seq"), None)
    return jax.shard_map(
        functools.partial(per_device, mesh.shape["seq"]),
        mesh=mesh,
        in_specs=(rows,) * 9 + (P(("groups", "seq")),),
        out_specs=(rows,) * 8,
        check_vma=False,
    )
```

```python
import functools
import math

import jax
import jax.numpy as jnp
from jax import lax
from jax.experimental import pallas as pl
from jax.experimental.pallas import tpu as pltpu
from jax.sharding import PartitionSpec as P

HEAD_DIM = 128
PAD = 16
MESH = pl.DeviceIdType.MESH
F32 = jnp.float32
BF16 = jnp.bfloat16


def dot(a, b, ca, cb):
    return lax.dot_general(a, b, (((ca,), (cb,)), ((), ())), preferred_element_type=F32)


def kernel(
    n, A, B, C, heads, seg, nb, win,
    q_ref, k_ref, v_ref, d_ref, qb_ref, kb_ref, vb_ref, db_ref, mask_ref, off_ref,
    o_t, o_b, gq_t, gk_t, gv_t, gq_b, gk_b, gv_b,
    G, KB, VB, TK, TV, SK, SV, RK, RV, WK, WV, QP, DP, bias,
    R, R1, S2, R2, X2, S3, R3,
    t_s, t_r, u_s, u_r, g1s, g1r, g2s, g2r, g3s, g3r, r1s, r1r, r2s, r2r, r3s, r3r,
):
    feat = heads * HEAD_DIM
    hc = heads // C
    hw = hc // 2
    w = hw * HEAD_DIM
    cw = hc * HEAD_DIM
    ratio = seg // nb
    cg = C // GC
    rows = seg + PAD
    scale = 1.0 / HEAD_DIM**0.5
    me = lax.axis_index("seq")
    c0 = lax.rem(me, 2)
    b0 = lax.rem(me // 2, B)
    a0 = me // (2 * B)

    def at(a, b, c):
        return {"seq": (a * B + b) * 2 + c}

    def remote(src, dst, ss, rs, dev):
        return pltpu.make_async_remote_copy(
            src_ref=src, dst_ref=dst, send_sem=ss, recv_sem=rs, device_id=dev, device_id_type=MESH
        )

    zdev = [None] + [at(lax.rem(a0 + d, A), b0, c0) for d in range(1, A)]
    ydev = [None] + [at(a0, lax.rem(b0 + d, B), c0) for d in range(1, B)]
    cdev = at(a0, b0, 1 - c0)

    barrier = pltpu.get_barrier_semaphore()
    for dev in zdev[1:] + ydev[1:] + [cdev]:
        pl.semaphore_signal(barrier, inc=1, device_id=dev, device_id_type=MESH)

    @pl.when(me > 0)
    def _():
        pl.semaphore_signal(barrier, inc=1, device_id={"seq": me - 1}, device_id_type=MESH)

    @pl.when(me < n - 1)
    def _():
        pl.semaphore_signal(barrier, inc=1, device_id={"seq": me + 1}, device_id_type=MESH)

    for c in range(C):
        parts = []
        for half in range(2):
            cols = slice(c * cw + half * w, c * cw + (half + 1) * w)
            parts += [kb_ref[:, cols].astype(F32), vb_ref[:, cols].astype(F32)]
        G[c // cg, c0, b0, a0, c % cg] = jnp.concatenate(parts, axis=0).astype(BF16)

    pl.semaphore_wait(barrier, A + B + 1 - (me == 0).astype(jnp.int32) - (me == n - 1).astype(jnp.int32))

    def hop1(g, d, src=0):
        return remote(
            G.at[g, c0, b0, a0], G.at[g, c0, b0, lax.rem(a0 + A - src, A)], g1s.at[g, d], g1r.at[g, d], zdev[d]
        )

    def hop2(g, d, src=0):
        return remote(
            G.at[g, c0, b0], G.at[g, c0, lax.rem(b0 + B - src, B)], g2s.at[g, d], g2r.at[g, d], ydev[d]
        )

    def hop3(g, src=0):
        return remote(G.at[g, c0], G.at[g, lax.rem(c0 + src, 2)], g3s.at[g], g3r.at[g], cdev)

    for g in range(GC):
        for d in range(1, A):
            hop1(g, d).start()

    def tail(x, c):
        src, dst = ((k_ref, TK), (v_ref, TV))[x]
        cols = pl.ds(c * cw, cw)
        return remote(
            src.at[pl.ds(seg - win, win), cols], dst.at[:, cols], t_s.at[x, c], t_r.at[x, c], {"seq": lax.rem(me + 1, n)}
        )

    def back(x, c):
        src, dst = ((SK, RK), (SV, RV))[x]
        cols = pl.ds(c * cw, cw)
        return remote(
            src.at[:, cols], dst.at[:, cols], u_s.at[x, c], u_r.at[x, c], {"seq": lax.rem(me + n - 1, n)}
        )

    def tail_start(c):
        @pl.when(me < n - 1)
        def _():
            tail(0, c).start()
            tail(1, c).start()

    tail_start(0)

    @pl.when(me == 0)
    def _():
        TK[...] = jnp.zeros_like(TK)
        TV[...] = jnp.zeros_like(TV)

    @pl.when(me == n - 1)
    def _():
        RK[...] = jnp.zeros_like(RK)
        RV[...] = jnp.zeros_like(RV)

    zpad = jnp.zeros((PAD - nb, feat), F32)
    QP[...] = jnp.concatenate([qb_ref[...].astype(F32), zpad], axis=0).astype(BF16)
    DP[...] = jnp.concatenate([db_ref[...].astype(F32), zpad], axis=0).astype(BF16)

    NEG = -1e30

    def ids(width):
        return (
            lax.broadcasted_iota(jnp.int32, (rows, width), 0),
            lax.broadcasted_iota(jnp.int32, (rows, width), 1),
        )

    r, u = ids(win)
    ok = (r < seg) & (u > r) & (me >= 1)
    bias[:, :win] = jnp.where(ok, 0.0, NEG)
    r, u = ids(seg)
    limit = jnp.where(r < seg, r, -1)
    for b in range(nb):
        limit = jnp.where(r == seg + b, b * ratio + off_ref[b], limit)
    low = jnp.where(r < seg, r - win, -1)
    bias[:, win : win + seg] = jnp.where((u <= limit) & (u > low), 0.0, NEG)
    r, u = ids(n * nb)
    slot = u // nb
    half_n = n // 2
    owner = ((slot % A) * B + (slot % half_n) // A) * 2 + slot // half_n
    one = owner[:1]
    opened = jnp.zeros((1, n * nb), jnp.int32)
    for j in range(n):
        opened = jnp.where(one == j, mask_ref[0, j], opened)
    opened = jnp.where(one < me, opened, 0)
    earlier = jnp.broadcast_to(opened, (rows, n * nb)) == 1
    mine = (owner == me) & (r >= seg) & (u % nb <= r - seg)
    bias[:, win + seg :] = jnp.where((earlier | mine) & (r < seg + nb), 0.0, NEG)

    for g in range(GC):
        for d in range(1, A):
            hop1(g, d, d).wait_recv()
        for d in range(1, B):
            hop2(g, d).start()
    for c in range(1, cg):
        tail_start(c)

    def assemble(g, m, carry):
        for c in range(g * cg, (g + 1) * cg):
            for half in range(2):
                cols = slice(c * cw + half * w, c * cw + (half + 1) * w)
                got = []
                for i in range(PAD // nb):
                    s = m * (PAD // nb) + i
                    got.append(
                        G[g, s // half_n, (s % half_n) // A, s % A, c % cg, half * 8 : half * 8 + 8, :].astype(F32)
                    )
                at_rows = pl.ds(pl.multiple_of(m * PAD, PAD), PAD)
                KB[at_rows, cols] = jnp.concatenate([x[:nb] for x in got], axis=0).astype(BF16)
                VB[at_rows, cols] = jnp.concatenate([x[nb:] for x in got], axis=0).astype(BF16)
        return carry

    def pass_on(g):
        for d in range(1, B):
            hop2(g, d, d).wait_recv()
        hop3(g).start()

    def arrived(g):
        hop3(g, 1).wait_recv()
        lax.fori_loop(0, n * nb // PAD, functools.partial(assemble, g), 0)

    c_exp = scale * math.log2(math.e)

    def head(c, l):
        h = c * hc + l
        cols = pl.ds(pl.multiple_of(h * HEAD_DIM, HEAD_DIM), HEAD_DIM)
        q = jnp.concatenate([q_ref[:, cols], QP[:, cols]], axis=0)
        d = jnp.concatenate([d_ref[:, cols], DP[:, cols]], axis=0)
        kk = jnp.concatenate([TK[:, cols], k_ref[:, cols], KB[:, cols]], axis=0)
        vv = jnp.concatenate([TV[:, cols], v_ref[:, cols], VB[:, cols]], axis=0)
        s = dot(q, kk, 1, 1) + bias[...]
        gp = dot(d, vv, 1, 1)
        e = jnp.exp2((s - jnp.max(s, axis=1, keepdims=True)) * c_exp)
        p = e * (1.0 / jnp.sum(e, axis=1, keepdims=True))
        wt = p.astype(BF16)
        o = dot(wt, vv, 1, 0).astype(BF16)
        delta = jnp.sum(d.astype(F32) * o.astype(F32), axis=1, keepdims=True)
        ds = (p * (gp - delta)).astype(BF16)
        gq = (dot(ds, kk, 1, 0) * scale).astype(BF16)
        gv = dot(wt, d, 0, 0)
        gk = dot(ds, q, 0, 0) * scale
        o_t[:, cols] = o[:seg]
        o_b[:, cols] = o[seg : seg + nb]
        gq_t[:, cols] = gq[:seg]
        gq_b[:, cols] = gq[seg : seg + nb]
        mid = seg
        SK[:, cols] = gk[:win].astype(BF16)
        SV[:, cols] = gv[:win].astype(BF16)
        gk_t[: seg - win, cols] = gk[win:mid].astype(BF16)
        gv_t[: seg - win, cols] = gv[win:mid].astype(BF16)
        WK[:, cols] = gk[mid : win + seg]
        WV[:, cols] = gv[mid : win + seg]
        half = l // hw
        rcols = pl.ds(pl.multiple_of((l % hw) * HEAD_DIM, HEAD_DIM), HEAD_DIM)
        rrows = pl.ds(pl.multiple_of(half * 8, 8), 8)
        for sl in range(n):
            lo = win + seg + sl * nb
            both = jnp.concatenate([gk[lo : lo + nb], gv[lo : lo + nb]], axis=0)
            R[c, sl // half_n, (sl % half_n) // A, sl % A, rrows, rcols] = both

    def red1(c):
        return remote(R.at[c, 1 - c0], R1.at[c], r1s.at[c], r1r.at[c], cdev)

    def red2(c, d):
        return remote(S2.at[c, lax.rem(b0 + d, B)], R2.at[c, d], r2s.at[c, d], r2r.at[c, d], ydev[d])

    def red3(c, d):
        return remote(S3.at[c, lax.rem(a0 + d, A)], R3.at[c, d], r3s.at[c, d], r3r.at[c, d], zdev[d])

    def step1(c):
        red1(c).wait_recv()
        for b in range(B):
            tot = R1[c, b] + R[c, c0, b]
            R1[c, b] = tot
            S2[c, b] = tot.astype(BF16)
        for d in range(1, B):
            red2(c, d).start()

    def step2(c):
        tot = R1[c, b0]
        for d in range(1, B):
            red2(c, d).wait_recv()
            tot = tot + R2[c, d].astype(F32)
        X2[c] = tot
        S3[c] = tot.astype(BF16)
        for d in range(1, A):
            red3(c, d).start()

    def step3(c):
        tot = X2[c, a0]
        for d in range(1, A):
            red3(c, d).wait_recv()
            tot = tot + R3[c, d].astype(F32)
        for half in range(2):
            cols = slice(c * cw + half * w, c * cw + (half + 1) * w)
            gk_b[:, cols] = tot[half * 8 : half * 8 + nb].astype(BF16)
            gv_b[:, cols] = tot[half * 8 + nb : half * 8 + 8].astype(BF16)

    pass_on(0)
    for c in range(cg, C):
        tail_start(c)
    for c in range(C):
        if c % cg == 0:
            arrived(c // cg)

        @pl.when(me > 0)
        def _():
            tail(0, c).wait_recv()
            tail(1, c).wait_recv()

        def one_head(l, carry):
            head(c, l)
            return carry

        lax.fori_loop(0, hc, one_head, 0, unroll=UNROLL)

        red1(c).start()

        @pl.when(me > 0)
        def _():
            back(0, c).start()
            back(1, c).start()

        if c % cg == 0 and c // cg + 1 < GC:
            pass_on(c // cg + 1)
        if c >= 1:
            step1(c - 1)
        if c >= 2:
            step2(c - 2)

    step1(C - 1)
    if C >= 2:
        step2(C - 2)
    step2(C - 1)

    for c in range(C):

        @pl.when(me < n - 1)
        def _():
            back(0, c).wait_recv()
            back(1, c).wait_recv()

        cols = slice(c * cw, (c + 1) * cw)
        gk_t[seg - win :, cols] = (WK[:, cols] + RK[:, cols].astype(F32)).astype(BF16)
        gv_t[seg - win :, cols] = (WV[:, cols] + RV[:, cols].astype(F32)).astype(BF16)

    for c in range(C):
        step3(c)

    for g in range(GC):
        for d in range(1, A):
            hop1(g, d).wait_send()
        for d in range(1, B):
            hop2(g, d).wait_send()
        hop3(g).wait_send()
    for c in range(C):
        red1(c).wait_send()
        for d in range(1, B):
            red2(c, d).wait_send()
        for d in range(1, A):
            red3(c, d).wait_send()

        @pl.when(me < n - 1)
        def _():
            tail(0, c).wait_send()
            tail(1, c).wait_send()

        @pl.when(me > 0)
        def _():
            back(0, c).wait_send()
            back(1, c).wait_send()


def hand_over(*refs):
    src, dst, held, ins, outs = refs[:8], refs[8:16], refs[16:24], refs[24], refs[25]
    first = [pltpu.make_async_copy(src[i], held[i], ins.at[i]) for i in range(8)]
    second = [pltpu.make_async_copy(held[i], dst[i], outs.at[i]) for i in range(8)]
    for copy in first:
        copy.start()
    for i in range(8):
        first[i].wait()
        second[i].start()
    for copy in second:
        copy.wait()


UNROLL = 4
GC = 2


def per_device(n, q, k, v, dout, qb, kb, vb, db, mask, off):
    seg, feat = q.shape
    nb = qb.shape[0]
    win = seg // 2
    heads = feat // HEAD_DIM
    chips = n // 2
    B = 2 ** (int(math.log2(chips)) // 2)
    A = chips // B
    C = 4
    w = heads // C // 2 * HEAD_DIM
    keys = win + seg + n * nb
    vm = pltpu.VMEM
    dma = pltpu.SemaphoreType.DMA
    scratch = [
        vm((GC, 2, B, A, C // GC, 16, w), BF16),
        vm((n * nb, feat), BF16),
        vm((n * nb, feat), BF16),
    ]
    scratch += [vm((win, feat), BF16)] * 6
    scratch += [vm((seg - win, feat), F32)] * 2
    scratch += [vm((PAD, feat), BF16)] * 2
    scratch += [vm((seg + PAD, keys), F32)]
    scratch += [
        vm((C, 2, B, A, 16, w), F32),
        vm((C, B, A, 16, w), F32),
        vm((C, B, A, 16, w), BF16),
        vm((C, B, A, 16, w), BF16),
        vm((C, A, 16, w), F32),
        vm((C, A, 16, w), BF16),
        vm((C, A, 16, w), BF16),
    ]
    scratch += [dma((2, C))] * 4 + [dma((GC, A))] * 2 + [dma((GC, B))] * 2 + [dma((GC,))] * 2
    scratch += [dma((C,))] * 2 + [dma((C, B))] * 2 + [dma((C, A))] * 2
    big = jax.ShapeDtypeStruct((seg, feat), BF16)
    small = jax.ShapeDtypeStruct((nb, feat), BF16)
    vspec = pl.BlockSpec(memory_space=pltpu.VMEM)
    sspec = pl.BlockSpec(memory_space=pltpu.SMEM)
    macs = (seg + PAD) * keys * feat * 5
    parts = pl.pallas_call(
        functools.partial(kernel, n, A, B, C, heads, seg, nb, win),
        out_shape=(big, small, big, big, big, small, small, small),
        in_specs=[vspec] * 8 + [sspec] * 2,
        out_specs=(vspec,) * 8,
        scratch_shapes=scratch,
        cost_estimate=pl.CostEstimate(
            flops=2 * macs, bytes_accessed=8 * seg * feat * 2, transcendentals=(seg + PAD) * keys * heads
        ),
        compiler_params=pltpu.CompilerParams(
            collective_id=0, has_side_effects=True, vmem_limit_bytes=56 * 1024 * 1024
        ),
    )(q, k, v, dout, qb, kb, vb, db, mask, off)
    aspec = pl.BlockSpec(memory_space=pl.ANY)
    return pl.pallas_call(
        hand_over,
        out_shape=(big, small, big, big, big, small, small, small),
        in_specs=[aspec] * 8,
        out_specs=(aspec,) * 8,
        scratch_shapes=[vm(x.shape, BF16) for x in (big, small, big, big, big, small, small, small)]
        + [dma((8,))] * 2,
        cost_estimate=pl.CostEstimate(flops=0, bytes_accessed=16 * seg * feat, transcendentals=0),
    )(*parts)


def solution(mesh):
    rows = P(("groups", "seq"), None)
    return jax.shard_map(
        functools.partial(per_device, mesh.shape["seq"]),
        mesh=mesh,
        in_specs=(rows,) * 9 + (P(("groups", "seq")),),
        out_specs=(rows,) * 8,
        check_vma=False,
    )
```

```python
import functools
import math

import jax
import jax.numpy as jnp
from jax import lax
from jax.experimental import pallas as pl
from jax.experimental.pallas import tpu as pltpu
from jax.sharding import PartitionSpec as P

HEAD_DIM = 128
PAD = 16
MESH = pl.DeviceIdType.MESH
F32 = jnp.float32
BF16 = jnp.bfloat16


def dot(a, b, ca, cb):
    return lax.dot_general(a, b, (((ca,), (cb,)), ((), ())), preferred_element_type=F32)


def kernel(
    n, C, heads, seg, nb, win,
    q_ref, k_ref, v_ref, d_ref, qb_ref, kb_ref, vb_ref, db_ref, mask_ref, off_ref,
    o_t, o_b, gq_t, gk_t, gv_t, gq_b, gk_b, gv_b,
    G, KB, VB, TK, TV, SK, SV, RK, RV, WK, WV, QP, DP, bias,
    R, R1, S2, R2,
    t_s, t_r, u_s, u_r, g1s, g1r, g2s, g2r, r1s, r1r, r2s, r2r,
):
    feat = heads * HEAD_DIM
    hc = heads // C
    hw = hc // 2
    w = hw * HEAD_DIM
    cw = hc * HEAD_DIM
    ratio = seg // nb
    cg = C // GC
    rows = seg + PAD
    scale = 1.0 / HEAD_DIM**0.5
    me = lax.axis_index("seq")
    c0 = lax.rem(me, 2)
    chips = n // 2
    p0 = me // 2
    cdev = {"seq": p0 * 2 + 1 - c0}

    def chip(d):
        return {"seq": lax.rem(p0 + d + chips, chips) * 2 + c0}

    def remote(src, dst, ss, rs, dev):
        return pltpu.make_async_remote_copy(
            src_ref=src, dst_ref=dst, send_sem=ss, recv_sem=rs, device_id=dev, device_id_type=MESH
        )

    barrier = pltpu.get_barrier_semaphore()
    for dev in [chip(d) for d in range(1, chips)] + [cdev]:
        pl.semaphore_signal(barrier, inc=1, device_id=dev, device_id_type=MESH)

    @pl.when(me > 0)
    def _():
        pl.semaphore_signal(barrier, inc=1, device_id={"seq": me - 1}, device_id_type=MESH)

    @pl.when(me < n - 1)
    def _():
        pl.semaphore_signal(barrier, inc=1, device_id={"seq": me + 1}, device_id_type=MESH)

    for c in range(C):
        parts = []
        for half in range(2):
            cols = slice(c * cw + half * w, c * cw + (half + 1) * w)
            parts += [kb_ref[:, cols].astype(F32), vb_ref[:, cols].astype(F32)]
        G[c // cg, c0, p0, c % cg] = jnp.concatenate(parts, axis=0).astype(BF16)

    pl.semaphore_wait(barrier, chips + 2 - (me == 0).astype(jnp.int32) - (me == n - 1).astype(jnp.int32))

    def up(g, d):
        return remote(G.at[g, c0, p0], G.at[g, c0, p0], g1s.at[g, d], g1r.at[g, d], chip(d))

    def up_here(g, d):
        slot = G.at[g, c0, lax.rem(p0 - d + chips, chips)]
        return remote(slot, slot, g1s.at[g, d], g1r.at[g, d], chip(d))

    def across(g, src=0):
        return remote(G.at[g, c0], G.at[g, lax.rem(c0 + src, 2)], g2s.at[g], g2r.at[g], cdev)

    def up_start(g):
        for d in range(1, chips):

            @pl.when(p0 + d < chips)
            def _():
                up(g, d).start()

    up_start(0)

    def tail(x, c):
        src, dst = ((k_ref, TK), (v_ref, TV))[x]
        cols = pl.ds(c * cw, cw)
        return remote(
            src.at[pl.ds(seg - win, win), cols], dst.at[:, cols], t_s.at[x, c], t_r.at[x, c], {"seq": lax.rem(me + 1, n)}
        )

    def back(x, c):
        src, dst = ((SK, RK), (SV, RV))[x]
        cols = pl.ds(c * cw, cw)
        return remote(
            src.at[:, cols], dst.at[:, cols], u_s.at[x, c], u_r.at[x, c], {"seq": lax.rem(me + n - 1, n)}
        )

    def tail_start(c):
        @pl.when(me < n - 1)
        def _():
            tail(0, c).start()
            tail(1, c).start()

    tail_start(0)
    for g in range(1, GC):
        up_start(g)

    for d in range(1, chips):

        @pl.when(p0 < d)
        def _():
            for g in range(GC):
                G[g, c0, p0 - d + chips] = jnp.zeros_like(G[g, c0, 0])

        @pl.when(p0 + d >= chips)
        def _():
            for c in range(C):
                R2[c, d] = jnp.zeros_like(R2[c, d])

    @pl.when(me == 0)
    def _():
        TK[...] = jnp.zeros_like(TK)
        TV[...] = jnp.zeros_like(TV)

    @pl.when(me == n - 1)
    def _():
        RK[...] = jnp.zeros_like(RK)
        RV[...] = jnp.zeros_like(RV)

    zpad = jnp.zeros((PAD - nb, feat), F32)
    QP[...] = jnp.concatenate([qb_ref[...].astype(F32), zpad], axis=0).astype(BF16)
    DP[...] = jnp.concatenate([db_ref[...].astype(F32), zpad], axis=0).astype(BF16)

    NEG = -1e30

    def ids(width):
        return (
            lax.broadcasted_iota(jnp.int32, (rows, width), 0),
            lax.broadcasted_iota(jnp.int32, (rows, width), 1),
        )

    r, u = ids(win)
    ok = (r < seg) & (u > r) & (me >= 1)
    bias[:, :win] = jnp.where(ok, 0.0, NEG)
    r, u = ids(seg)
    limit = jnp.where(r < seg, r, -1)
    for b in range(nb):
        limit = jnp.where(r == seg + b, b * ratio + off_ref[b], limit)
    low = jnp.where(r < seg, r - win, -1)
    bias[:, win : win + seg] = jnp.where((u <= limit) & (u > low), 0.0, NEG)
    r, u = ids(n * nb)
    slot = u // nb
    owner = (slot % chips) * 2 + slot // chips
    one = owner[:1]
    opened = jnp.zeros((1, n * nb), jnp.int32)
    for j in range(n):
        opened = jnp.where(one == j, mask_ref[0, j], opened)
    opened = jnp.where(one < me, opened, 0)
    earlier = jnp.broadcast_to(opened, (rows, n * nb)) == 1
    mine = (owner == me) & (r >= seg) & (u % nb <= r - seg)
    bias[:, win + seg :] = jnp.where((earlier | mine) & (r < seg + nb), 0.0, NEG)

    def assemble(g, m, carry):
        for c in range(g * cg, (g + 1) * cg):
            for half in range(2):
                cols = slice(c * cw + half * w, c * cw + (half + 1) * w)
                got = []
                for i in range(PAD // nb):
                    s = m * (PAD // nb) + i
                    got.append(
                        G[g, s // chips, s % chips, c % cg, half * 8 : half * 8 + 8, :].astype(F32)
                    )
                at_rows = pl.ds(pl.multiple_of(m * PAD, PAD), PAD)
                KB[at_rows, cols] = jnp.concatenate([x[:nb] for x in got], axis=0).astype(BF16)
                VB[at_rows, cols] = jnp.concatenate([x[nb:] for x in got], axis=0).astype(BF16)
        return carry

    def pass_on(g):
        for d in range(1, chips):

            @pl.when(p0 >= d)
            def _():
                up_here(g, d).wait_recv()

        across(g).start()

    def arrived(g):
        across(g, 1).wait_recv()
        lax.fori_loop(0, n * nb // PAD, functools.partial(assemble, g), 0)

    c_exp = scale * math.log2(math.e)

    def head(c, l):
        h = c * hc + l
        cols = pl.ds(pl.multiple_of(h * HEAD_DIM, HEAD_DIM), HEAD_DIM)
        q = jnp.concatenate([q_ref[:, cols], QP[:, cols]], axis=0)
        d = jnp.concatenate([d_ref[:, cols], DP[:, cols]], axis=0)
        kk = jnp.concatenate([TK[:, cols], k_ref[:, cols], KB[:, cols]], axis=0)
        vv = jnp.concatenate([TV[:, cols], v_ref[:, cols], VB[:, cols]], axis=0)
        s = dot(q, kk, 1, 1) + bias[...]
        gp = dot(d, vv, 1, 1)
        e = jnp.exp2((s - jnp.max(s, axis=1, keepdims=True)) * c_exp)
        p = e * (1.0 / jnp.sum(e, axis=1, keepdims=True))
        wt = p.astype(BF16)
        o = dot(wt, vv, 1, 0).astype(BF16)
        delta = jnp.sum(d.astype(F32) * o.astype(F32), axis=1, keepdims=True)
        ds = (p * (gp - delta)).astype(BF16)
        gq = (dot(ds, kk, 1, 0) * scale).astype(BF16)
        gv = dot(wt, d, 0, 0)
        gk = dot(ds, q, 0, 0) * scale
        o_t[:, cols] = o[:seg]
        o_b[:, cols] = o[seg : seg + nb]
        gq_t[:, cols] = gq[:seg]
        gq_b[:, cols] = gq[seg : seg + nb]
        mid = seg
        SK[:, cols] = gk[:win].astype(BF16)
        SV[:, cols] = gv[:win].astype(BF16)
        gk_t[: seg - win, cols] = gk[win:mid].astype(BF16)
        gv_t[: seg - win, cols] = gv[win:mid].astype(BF16)
        WK[:, cols] = gk[mid : win + seg]
        WV[:, cols] = gv[mid : win + seg]
        half = l // hw
        rcols = pl.ds(pl.multiple_of((l % hw) * HEAD_DIM, HEAD_DIM), HEAD_DIM)
        rrows = pl.ds(pl.multiple_of(half * 8, 8), 8)
        for sl in range(n):
            lo = win + seg + sl * nb
            both = jnp.concatenate([gk[lo : lo + nb], gv[lo : lo + nb]], axis=0)
            R[c, sl // chips, sl % chips, rrows, rcols] = both

    def red1(c):
        return remote(R.at[c, 1 - c0], R1.at[c], r1s.at[c], r1r.at[c], cdev)

    def down(c, d):
        return remote(
            S2.at[c, lax.rem(p0 - d + chips, chips)], R2.at[c, d], r2s.at[c, d], r2r.at[c, d], chip(-d)
        )

    def step1(c):
        red1(c).wait_recv()
        tot = R1[c] + R[c, c0]
        R1[c] = tot
        S2[c] = tot.astype(BF16)
        for d in range(1, chips):

            @pl.when(p0 >= d)
            def _():
                down(c, d).start()

    def step2(c):
        for d in range(1, chips):

            @pl.when(p0 + d < chips)
            def _():
                down(c, d).wait_recv()

        tot = R1[c, p0]
        for d in range(1, chips):
            tot = tot + R2[c, d].astype(F32)
        for half in range(2):
            cols = slice(c * cw + half * w, c * cw + (half + 1) * w)
            gk_b[:, cols] = tot[half * 8 : half * 8 + nb].astype(BF16)
            gv_b[:, cols] = tot[half * 8 + nb : half * 8 + 8].astype(BF16)

    pass_on(0)
    for c in range(1, C):
        tail_start(c)
    for c in range(C):
        if c % cg == 0:
            arrived(c // cg)

        @pl.when(me > 0)
        def _():
            tail(0, c).wait_recv()
            tail(1, c).wait_recv()

        def one_head(l, carry):
            head(c, l)
            return carry

        lax.fori_loop(0, hc, one_head, 0, unroll=UNROLL)

        red1(c).start()

        @pl.when(me > 0)
        def _():
            back(0, c).start()
            back(1, c).start()

        if c % cg == 0 and c // cg + 1 < GC:
            pass_on(c // cg + 1)
        if c >= 1:
            step1(c - 1)

    step1(C - 1)

    for c in range(C):

        @pl.when(me < n - 1)
        def _():
            back(0, c).wait_recv()
            back(1, c).wait_recv()

        cols = slice(c * cw, (c + 1) * cw)
        gk_t[seg - win :, cols] = (WK[:, cols] + RK[:, cols].astype(F32)).astype(BF16)
        gv_t[seg - win :, cols] = (WV[:, cols] + RV[:, cols].astype(F32)).astype(BF16)

    for c in range(C):
        step2(c)

    for g in range(GC):
        for d in range(1, chips):

            @pl.when(p0 + d < chips)
            def _():
                up(g, d).wait_send()

        across(g).wait_send()
    for c in range(C):
        red1(c).wait_send()
        for d in range(1, chips):

            @pl.when(p0 >= d)
            def _():
                down(c, d).wait_send()

        @pl.when(me < n - 1)
        def _():
            tail(0, c).wait_send()
            tail(1, c).wait_send()

        @pl.when(me > 0)
        def _():
            back(0, c).wait_send()
            back(1, c).wait_send()


def hand_over(*refs):
    src, dst, held, ins, outs = refs[:8], refs[8:16], refs[16:24], refs[24], refs[25]
    first = [pltpu.make_async_copy(src[i], held[i], ins.at[i]) for i in range(8)]
    second = [pltpu.make_async_copy(held[i], dst[i], outs.at[i]) for i in range(8)]
    for copy in first:
        copy.start()
    for i in range(8):
        first[i].wait()
        second[i].start()
    for copy in second:
        copy.wait()


UNROLL = 4
GC = 2


def per_device(n, q, k, v, dout, qb, kb, vb, db, mask, off):
    seg, feat = q.shape
    nb = qb.shape[0]
    win = seg // 2
    heads = feat // HEAD_DIM
    chips = n // 2
    C = 4
    w = heads // C // 2 * HEAD_DIM
    keys = win + seg + n * nb
    vm = pltpu.VMEM
    dma = pltpu.SemaphoreType.DMA
    scratch = [
        vm((GC, 2, chips, C // GC, 16, w), BF16),
        vm((n * nb, feat), BF16),
        vm((n * nb, feat), BF16),
    ]
    scratch += [vm((win, feat), BF16)] * 6
    scratch += [vm((seg - win, feat), F32)] * 2
    scratch += [vm((PAD, feat), BF16)] * 2
    scratch += [vm((seg + PAD, keys), F32)]
    scratch += [
        vm((C, 2, chips, 16, w), F32),
        vm((C, chips, 16, w), F32),
        vm((C, chips, 16, w), BF16),
        vm((C, chips, 16, w), BF16),
    ]
    scratch += [dma((2, C))] * 4 + [dma((GC, chips))] * 2 + [dma((GC,))] * 2
    scratch += [dma((C,))] * 2 + [dma((C, chips))] * 2
    big = jax.ShapeDtypeStruct((seg, feat), BF16)
    small = jax.ShapeDtypeStruct((nb, feat), BF16)
    vspec = pl.BlockSpec(memory_space=pltpu.VMEM)
    sspec = pl.BlockSpec(memory_space=pltpu.SMEM)
    macs = (seg + PAD) * keys * feat * 5
    parts = pl.pallas_call(
        functools.partial(kernel, n, C, heads, seg, nb, win),
        out_shape=(big, small, big, big, big, small, small, small),
        in_specs=[vspec] * 8 + [sspec] * 2,
        out_specs=(vspec,) * 8,
        scratch_shapes=scratch,
        cost_estimate=pl.CostEstimate(
            flops=2 * macs, bytes_accessed=8 * seg * feat * 2, transcendentals=(seg + PAD) * keys * heads
        ),
        compiler_params=pltpu.CompilerParams(
            collective_id=0, has_side_effects=True, vmem_limit_bytes=56 * 1024 * 1024
        ),
    )(q, k, v, dout, qb, kb, vb, db, mask, off)
    aspec = pl.BlockSpec(memory_space=pl.ANY)
    return pl.pallas_call(
        hand_over,
        out_shape=(big, small, big, big, big, small, small, small),
        in_specs=[aspec] * 8,
        out_specs=(aspec,) * 8,
        scratch_shapes=[vm(x.shape, BF16) for x in (big, small, big, big, big, small, small, small)]
        + [dma((8,))] * 2,
        cost_estimate=pl.CostEstimate(flops=0, bytes_accessed=16 * seg * feat, transcendentals=0),
    )(*parts)


def solution(mesh):
    rows = P(("groups", "seq"), None)
    return jax.shard_map(
        functools.partial(per_device, mesh.shape["seq"]),
        mesh=mesh,
        in_specs=(rows,) * 9 + (P(("groups", "seq")),),
        out_specs=(rows,) * 8,
        check_vma=False,
    )
```
